32 devices in a mesh: row: 16 (over z, x, core), col: 2 (over y).
Axes of the slice: x: 2, y: 2, z: 4, core: 2. Of those that a mesh axis runs over, the one named last changes fastest.
Arguments:
- trail_adjoint: float32 [16, 128, 2, 1024], P('row', None, 'col'), may hold values from -2.8 to 2.8, as said below
- panel_one: float32 [2048, 512], P(('row', 'col')), may hold values from -0.125 to 0.125
- panel_two: float32 [2048, 512], P(('row', 'col')), may hold values from -0.125 to 0.125
- upstream_one: float32 [2048, 512], P(('row', 'col')), may hold values from -6 to 6
- upstream_two: float32 [2048, 512], P(('row', 'col')), may hold values from -6 to 6
- pivot_one: float32 [512, 512], replicated, may hold values from -1 to 2, as said below
- pivot_two: float32 [512, 512], replicated, may hold values from -1 to 2, as said below
- link_block: float32 [512, 512], replicated, may hold values from -0.25 to 0.25
- pivot_adjoint: float32 [2, 512, 512], replicated, may hold values from -6 to 6
Outputs:
- strip_grad_one: float32 [2048, 512], P(('row', 'col'))
- strip_grad_two: float32 [2048, 512], P(('row', 'col'))
- block_grads: float32 [3, 512, 512], replicated
The draws below stay inside these ranges and needn't reach their ends.
Inputs may be any that keep to these rules, and one draw needn't show every extreme that they name: trail_adjoint[a, c * 64 + s, c2, a2 * 64 + s2] equals trail_adjoint[a2, c2 * 64 + s2, c, a * 64 + s], so sbar is symmetric. `pivot_one`: lower triangular, diagonal entries between 1 and 2. `pivot_two`: lower triangular, diagonal entries between 1 and 2.
All inputs are finite; a program needn't handle non-finite values.
Results may differ from the reference program's by a relative error of at most 0.000062.
Values sent between devices are 32-bit elements; how exact they have to be, the bound alone decides.
A program may use at most 128 MiB of HBM per device.

```python
import math
import jax
import jax.numpy as jnp
from jax import lax

PANEL_WIDTH = 512
SLAB_ROWS = 64
GRID_ROWS = 16
GRID_COLS = 2
TRAIL_ROWS = 2048


def lower_factor(base_key):
    diag_key, off_key = jax.random.split(base_key)
    diagonal = jax.random.uniform(diag_key, (PANEL_WIDTH,), jnp.float32, 1.0, 2.0)
    strict_part = jnp.clip(jax.random.normal(off_key, (PANEL_WIDTH, PANEL_WIDTH), jnp.float32), -4.0, 4.0)
    strict_part = strict_part * (0.45 / math.sqrt(PANEL_WIDTH))
    return jnp.tril(strict_part, -1) + jnp.diag(diagonal)


def draw_pivot_one(key, part):
    return lower_factor(jax.random.fold_in(key, 11))


def draw_pivot_two(key, part):
    return lower_factor(jax.random.fold_in(key, 23))


def draw_trail_adjoint(key, part):
    shape_six = (GRID_ROWS, GRID_COLS, SLAB_ROWS, GRID_COLS, GRID_ROWS, SLAB_ROWS)
    raw_values = jnp.clip(jax.random.normal(jax.random.fold_in(key, 37), shape_six, jnp.float32), -4.0, 4.0) * 0.7
    mirrored = 0.5 * (raw_values + jnp.transpose(raw_values, (4, 3, 5, 1, 0, 2)))
    return mirrored.reshape(GRID_ROWS, GRID_COLS * SLAB_ROWS, GRID_COLS, GRID_ROWS * SLAB_ROWS)


def block_scale(rng, dims, cuts, low, high):
    loudness, own = 1.0, jax.random.fold_in(rng, 6)
    for axis_at, blocks in cuts:
        heights = jnp.exp(jax.random.uniform(jax.random.fold_in(own, axis_at), (blocks,), jnp.float32, low / len(cuts), high / len(cuts)))
        loudness = loudness * jnp.repeat(heights, dims[axis_at] // blocks).reshape([-1 if axis == axis_at else 1 for axis in range(len(dims))])
    return loudness


def scatter_about(key, extent, scale, bound, cuts=(), kind=jnp.bfloat16):
    drawn = jax.random.normal(key, extent, jnp.float32) * scale
    if len(cuts) > 0:
        drawn = block_scale(key, extent, cuts, -0.22, 0.18) * drawn
    return jnp.clip(drawn, min=-bound, max=bound).astype(kind)


def setup_inputs(seed: int = 0) -> dict:
    arg_keys = jax.random.split(jax.random.key(seed), 10)
    return {
        "trail_adjoint": draw_trail_adjoint(jax.random.fold_in(arg_keys[9], 71), 0),
        "panel_one": scatter_about(arg_keys[1], (TRAIL_ROWS, PANEL_WIDTH), TRAIL_ROWS ** -0.5, 0.125, ((0, 32),), jnp.float32),
        "panel_two": scatter_about(arg_keys[2], (TRAIL_ROWS, PANEL_WIDTH), TRAIL_ROWS ** -0.5, 0.125, ((0, 32),), jnp.float32),
        "upstream_one": scatter_about(arg_keys[3], (TRAIL_ROWS, PANEL_WIDTH), 1.0, 6.0, ((0, 32),), jnp.float32),
        "upstream_two": scatter_about(arg_keys[4], (TRAIL_ROWS, PANEL_WIDTH), 1.0, 6.0, ((0, 32),), jnp.float32),
        "pivot_one": draw_pivot_one(jax.random.fold_in(arg_keys[9], 71), 0),
        "pivot_two": draw_pivot_two(jax.random.fold_in(arg_keys[9], 71), 0),
        "link_block": scatter_about(arg_keys[7], (PANEL_WIDTH, PANEL_WIDTH), PANEL_WIDTH ** -0.5, 0.25, (), jnp.float32),
        "pivot_adjoint": scatter_about(arg_keys[8], (2, PANEL_WIDTH, PANEL_WIDTH), 1.0, 6.0, (), jnp.float32),
    }


def exact_dot(left, right):
    return jnp.dot(left.astype(jnp.float32), right.astype(jnp.float32), precision=lax.Precision.HIGHEST, preferred_element_type=jnp.float32)

def cross_dot(left, right):
    return lax.dot_general(left.astype(jnp.float32), right.astype(jnp.float32), (((0,), (0,)), ((), ())), precision=lax.Precision.HIGHEST, preferred_element_type=jnp.float32)

def lower_inverse(factor):
    identity = jnp.eye(factor.shape[0], dtype=jnp.float32)
    return jax.scipy.linalg.solve_triangular(factor, identity, lower=True)

def chol_grad(factor, cotangent, inverse):
    product = cross_dot(factor, jnp.tril(cotangent))
    halved = jnp.tril(product) - 0.5 * jnp.diag(jnp.diag(product))
    inner = cross_dot(inverse, exact_dot(halved, inverse))
    return 0.5 * (inner + inner.T)

def reference(trail_adjoint, panel_one, panel_two, upstream_one, upstream_two, pivot_one, pivot_two, link_block, pivot_adjoint):
    width = panel_one.shape[1]
    stacked = jnp.concatenate([panel_one, panel_two], axis=1)
    reordered = stacked.reshape(GRID_ROWS, GRID_COLS, SLAB_ROWS, 2 * width)
    reordered = jnp.transpose(reordered, (1, 0, 2, 3)).reshape(GRID_COLS, GRID_ROWS * SLAB_ROWS, 2 * width)

    def outer_block(slab_block):
        return 2.0 * jnp.einsum('pcq,cqk->pk', slab_block, reordered, precision=lax.Precision.HIGHEST)
    carried = lax.map(outer_block, trail_adjoint).reshape(TRAIL_ROWS, 2 * width)
    pressed_one = upstream_one - carried[:, :width]
    pressed_two = upstream_two - carried[:, width:]
    inverse_one = lower_inverse(pivot_one)
    inverse_two = lower_inverse(pivot_two)
    grad_two = exact_dot(pressed_two, inverse_two)
    cross_two = cross_dot(grad_two, panel_two)
    cross_link = cross_dot(grad_two, panel_one)
    grad_one = exact_dot(pressed_one - exact_dot(grad_two, link_block), inverse_one)
    cross_one = cross_dot(grad_one, panel_one)
    pivot_grad_two = chol_grad(pivot_two, pivot_adjoint[1] - cross_two, inverse_two)
    link_grad = -cross_link - 2.0 * exact_dot(pivot_grad_two, link_block)
    link_input = exact_dot(link_grad, inverse_one)
    pivot_grad_one = chol_grad(pivot_one, pivot_adjoint[0] - cross_dot(link_input, link_block) - cross_one, inverse_one)
    return (grad_one, grad_two, jnp.stack([pivot_grad_one, link_input, pivot_grad_two]))
```

```python
import jax
import jax.numpy as jnp
from jax import lax
from jax.experimental import pallas as pl
from jax.experimental.pallas import tpu as pltpu
from jax.sharding import PartitionSpec as P

TILE = 128
BASE = 8


def dot(left, right, precision=lax.Precision.HIGHEST):
    return jnp.dot(left, right, precision=precision, preferred_element_type=jnp.float32)


def high(left, right):
    return dot(left, right, lax.Precision.HIGH)


def tile_inverses(tiles):
    size = tiles[0].shape[0]
    row = lax.broadcasted_iota(jnp.int32, (size, size), 0)
    col = lax.broadcasted_iota(jnp.int32, (size, size), 1)
    eye = row == col
    one = jnp.where(eye, 1.0, 0.0)
    base = (row // BASE == col // BASE) & (row > col)
    nil, across = [], []
    for tile in tiles:
        diag = jnp.where(eye, tile, 0.0)
        down = 1.0 / jnp.sum(diag, axis=1, keepdims=True)
        across.append(1.0 / jnp.sum(diag, axis=0, keepdims=True))
        nil.append(jnp.where(base, -tile * down, 0.0))
    found = [one + n for n in nil]
    power = nil
    reach = 2
    while reach < BASE:
        power = [dot(p, p) for p in power]
        found = [f + dot(f, p) for f, p in zip(found, power)]
        reach *= 2
    found = [f * a for f, a in zip(found, across)]
    step = BASE
    while step < size:
        level = (row // (2 * step) == col // (2 * step)) & (row // step != col // step) & (row > col)
        below = [dot(jnp.where(level, t, 0.0), f) for t, f in zip(tiles, found)]
        found = [f - dot(f, b) for f, b in zip(found, below)]
        step *= 2
    return found


def invert(factors, outs):
    width = factors[0].shape[0]
    count = width // TILE
    tiles = [f[pl.ds(t * TILE, TILE), pl.ds(t * TILE, TILE)] for f in factors for t in range(count)]
    found = tile_inverses(tiles)
    for i, out in enumerate(outs):
        out[...] = jnp.zeros_like(out)
        for t in range(count):
            out[pl.ds(t * TILE, TILE), pl.ds(t * TILE, TILE)] = found[i * count + t]
    step = TILE
    while step < width:
        for at in range(0, width, 2 * step):
            top, low = pl.ds(at, step), pl.ds(at + step, step)
            belows = [dot(f[low, top], o[top, top]) for f, o in zip(factors, outs)]
            for o, b in zip(outs, belows):
                o[low, top] = -dot(o[low, low], b)
        step *= 2


def prepare(one_ref, two_ref, link_ref, adj_ref, inv_one, inv_two, inv_one_t, inv_two_t, mixed, mixed_t, adj_one, adj_two):
    invert((one_ref, two_ref), (inv_one, inv_two))
    inv_one_t[...] = inv_one[...].T
    inv_two_t[...] = inv_two[...].T
    mixed[...] = high(inv_two[...], link_ref[...])
    mixed_t[...] = mixed[...].T
    adj_one[...] = high(one_ref[...].T, adj_ref[0])
    adj_two[...] = high(two_ref[...].T, adj_ref[1])


def half_symmetric(x):
    row = lax.broadcasted_iota(jnp.int32, x.shape, 0)
    col = lax.broadcasted_iota(jnp.int32, x.shape, 1)
    return 0.5 * (jnp.where(row > col, x, 0.0) + jnp.where(row >= col, x, 0.0).T)


def finish(sums, inv_one, inv_two, inv_one_t, inv_two_t, mixed, mixed_t, adj_one, adj_two, out):
    sym_two = half_symmetric(adj_two[...] - sums[2])
    out[2] = high(inv_two_t[...], high(sym_two, inv_two[...]))
    turned = high(sym_two, mixed[...])
    out[1] = high(high(-inv_two_t[...], sums[1] + 2.0 * turned), inv_one[...])
    cross = high(mixed_t[...], sums[1] + turned)
    sym_one = half_symmetric(adj_one[...] - sums[0]) + 0.5 * (cross + cross.T)
    out[0] = high(inv_one_t[...], high(sym_one, inv_one[...]))


def whole(count):
    return [pl.BlockSpec(memory_space=pltpu.VMEM)] * count


def local(
    trail_adjoint,
    panel_one,
    panel_two,
    upstream_one,
    upstream_two,
    pivot_one,
    pivot_two,
    link_block,
    pivot_adjoint,
):
    width = panel_one.shape[1]
    square = jax.ShapeDtypeStruct((width, width), jnp.float32)
    params = pltpu.CompilerParams(vmem_limit_bytes=48 << 20)
    cost = pl.CostEstimate(flops=16 * width**3, bytes_accessed=48 * width**2, transcendentals=0)
    prepared = pl.pallas_call(
        prepare,
        out_shape=[square] * 8,
        in_specs=whole(4),
        out_specs=whole(8),
        compiler_params=params,
        cost_estimate=cost,
        name="prepare",
    )(pivot_one, pivot_two, link_block, pivot_adjoint)
    inverse_one, inverse_two = prepared[:2]
    stacked = jnp.concatenate([panel_one, panel_two], axis=1)
    matrix = trail_adjoint.reshape(trail_adjoint.shape[1], trail_adjoint.shape[3])
    summed = high(matrix, lax.all_gather(stacked, "row", axis=0, tiled=True))
    carried = lax.psum_scatter(2.0 * summed, "col", scatter_dimension=0, tiled=True)
    pressed_one = upstream_one - carried[:, :width]
    pressed_two = upstream_two - carried[:, width:]
    sums = lax.psum(
        jnp.stack(
            [
                high(pressed_one.T, panel_one),
                high(pressed_two.T, panel_one),
                high(pressed_two.T, panel_two),
            ]
        ),
        ("row", "col"),
    )
    grad_two = high(pressed_two, inverse_two)
    grad_one = high(pressed_one - high(grad_two, link_block), inverse_one)
    grads = pl.pallas_call(
        finish,
        out_shape=jax.ShapeDtypeStruct((3, width, width), jnp.float32),
        in_specs=whole(9),
        out_specs=pl.BlockSpec(memory_space=pltpu.VMEM),
        compiler_params=params,
        cost_estimate=cost,
        name="finish",
    )(sums, *prepared)
    return grad_one, grad_two, grads


def solution(mesh):
    return jax.shard_map(
        local,
        mesh=mesh,
        in_specs=(
            P("row", None, "col", None),
            P(("row", "col"), None),
            P(("row", "col"), None),
            P(("row", "col"), None),
            P(("row", "col"), None),
            P(),
            P(),
            P(),
            P(),
        ),
        out_specs=(P(("row", "col"), None), P(("row", "col"), None), P()),
        check_vma=False,
    )
```

```python
import functools

import jax
import jax.numpy as jnp
from jax import lax
from jax.experimental import pallas as pl
from jax.experimental.pallas import tpu as pltpu
from jax.sharding import PartitionSpec as P

TILE = 128
BASE = 8
CORES = 2
SIDE = 2


def dot(left, right, precision=lax.Precision.HIGHEST):
    return jnp.dot(left, right, precision=precision, preferred_element_type=jnp.float32)


def high(left, right):
    return dot(left, right, lax.Precision.HIGH)


def tile_inverses(tiles):
    size = tiles[0].shape[0]
    row = lax.broadcasted_iota(jnp.int32, (size, size), 0)
    col = lax.broadcasted_iota(jnp.int32, (size, size), 1)
    eye = row == col
    one = jnp.where(eye, 1.0, 0.0)
    base = (row // BASE == col // BASE) & (row > col)
    nil, across = [], []
    for tile in tiles:
        diag = jnp.where(eye, tile, 0.0)
        down = 1.0 / jnp.sum(diag, axis=1, keepdims=True)
        across.append(1.0 / jnp.sum(diag, axis=0, keepdims=True))
        nil.append(jnp.where(base, -tile * down, 0.0))
    found = [one + n for n in nil]
    power = nil
    reach = 2
    while reach < BASE:
        power = [dot(p, p) for p in power]
        found = [f + dot(f, p) for f, p in zip(found, power)]
        reach *= 2
    found = [f * a for f, a in zip(found, across)]
    step = BASE
    while step < size:
        level = (row // (2 * step) == col // (2 * step)) & (row // step != col // step) & (row > col)
        below = [dot(jnp.where(level, t, 0.0), f) for t, f in zip(tiles, found)]
        found = [f - dot(f, b) for f, b in zip(found, below)]
        step *= 2
    return found


def place_tiles(factors, outs):
    width = factors[0].shape[0]
    count = width // TILE
    spans = [pl.ds(t * TILE, TILE) for t in range(count)]
    found = tile_inverses([f[s, s] for f in factors for s in spans])
    for i, out in enumerate(outs):
        out[...] = jnp.zeros_like(out)
        for t, s in enumerate(spans):
            out[s, s] = found[i * count + t]


def join_tiles(factors, outs):
    width = factors[0].shape[0]
    step = TILE
    while step < width:
        for at in range(0, width, 2 * step):
            top, low = pl.ds(at, step), pl.ds(at + step, step)
            belows = [dot(f[low, top], o[top, top]) for f, o in zip(factors, outs)]
            for o, b in zip(outs, belows):
                o[low, top] = -dot(o[low, low], b)
        step *= 2


def half_symmetric(x):
    row = lax.broadcasted_iota(jnp.int32, x.shape, 0)
    col = lax.broadcasted_iota(jnp.int32, x.shape, 1)
    return 0.5 * (jnp.where(row > col, x, 0.0) + jnp.where(row >= col, x, 0.0).T)


def finish(sums, inv_one, inv_two, inv_one_t, inv_two_t, mixed, mixed_t, adj_one, adj_two, out):
    sym_two = half_symmetric(adj_two[...] - sums[2])
    out[2] = high(inv_two_t[...], high(sym_two, inv_two[...]))
    turned = high(sym_two, mixed[...])
    out[1] = high(high(-inv_two_t[...], sums[1] + 2.0 * turned), inv_one[...])
    cross = high(mixed_t[...], sums[1] + turned)
    sym_one = half_symmetric(adj_one[...] - sums[0]) + 0.5 * (cross + cross.T)
    out[0] = high(inv_one_t[...], high(sym_one, inv_one[...]))


class Spread:
    def __init__(self, buf, rows, send, recv):
        self.buf, self.send, self.recv = buf, send, recv
        self.r, self.c = lax.axis_index("row"), lax.axis_index("col")
        self.depth = rows // (SIDE * CORES)
        self.z = self.r // (SIDE * CORES)
        core, side = self.r % CORES, self.r // CORES % SIDE
        self.core_peer = self.r + 1 - 2 * core
        self.side_peer = self.r + CORES - 2 * CORES * side
        self.hop = SIDE * CORES
        self.sent = []

    def copy(self, block, way, target):
        return pltpu.make_async_remote_copy(
            src_ref=self.buf.at[block],
            dst_ref=self.buf.at[block],
            send_sem=self.send.at[way, block],
            recv_sem=self.recv.at[block],
            device_id=(target, self.c),
            device_id_type=pl.DeviceIdType.MESH,
        )

    def pass_on(self, block, way, target, when):
        @pl.when(when)
        def _():
            self.copy(block, way, target).start()

        self.sent.append((block, way, target, when))

    def await_block(self, block, when):
        @pl.when(when)
        def _():
            self.copy(block, 0, self.core_peer).wait_recv()

    def begin(self):
        r, z = self.r, self.z
        self.pass_on(r, 0, r + self.hop, z < self.depth - 1)
        self.pass_on(r, 1, r - self.hop, z > 0)
        self.pass_on(r, 2, self.side_peer, z >= 0)
        self.pass_on(r, 3, self.core_peer, z >= 0)

    def origins(self, step):
        if step == 0:
            return [(0, self.z >= 0)]
        return [(-step, self.z >= step), (step, self.z < self.depth - step)]

    def along(self, step):
        z, hop = self.z, self.hop
        for away, there in self.origins(step):
            block = self.r + away * hop
            self.await_block(block, there)
            if away < 0:
                self.pass_on(block, 0, self.r + hop, there & (z < self.depth - 1))
            else:
                self.pass_on(block, 1, self.r - hop, there & (z > 0))
            self.pass_on(block, 2, self.side_peer, there)
            self.pass_on(block, 3, self.core_peer, there)

    def across(self, step):
        for away, there in self.origins(step):
            block = self.side_peer + away * self.hop
            self.await_block(block, there)
            self.pass_on(block, 3, self.core_peer, there)

    def other_core(self, step):
        for away, there in self.origins(step):
            self.await_block(self.core_peer + away * self.hop, there)
            flipped = self.side_peer + self.core_peer - self.r
            self.await_block(flipped + away * self.hop, there)

    def end(self):
        for block, way, target, when in self.sent:
            @pl.when(when)
            def _():
                self.copy(block, way, target).wait_send()


def to_peer(src, dst, send, recv, target):
    return pltpu.make_async_remote_copy(
        src_ref=src,
        dst_ref=dst,
        send_sem=send,
        recv_sem=recv,
        device_id=target,
        device_id_type=pl.DeviceIdType.MESH,
    )


def sweep(
    rows,
    cols,
    matrix,
    panel_one,
    panel_two,
    up_one,
    up_two,
    one_ref,
    two_ref,
    link_ref,
    adj_ref,
    grad_one,
    grad_two,
    sums,
    inv_one,
    inv_two,
    inv_one_t,
    inv_two_t,
    mixed,
    mixed_t,
    adj_one,
    adj_two,
    held,
    total,
    landed,
    pressed,
    outgoing,
    incoming,
    turned,
    part,
    parts,
    send_panels,
    recv_panels,
    send_carried,
    recv_carried,
    send_slices,
    recv_slices,
    send_part,
    recv_part,
    send_sums,
    recv_sums,
):
    r, c = lax.axis_index("row"), lax.axis_index("col")
    slab, width = panel_one.shape
    share = width // rows
    held[r, :, pl.ds(0, width)] = panel_one[...]
    held[r, :, pl.ds(width, width)] = panel_two[...]

    barrier = pltpu.get_barrier_semaphore()

    @pl.loop(1, rows)
    def _(i):
        pl.semaphore_signal(barrier, inc=1, device_id=(lax.rem(r + i, rows), c), device_id_type=pl.DeviceIdType.MESH)

    for i in range(1, cols):
        pl.semaphore_signal(barrier, inc=1, device_id=(r, lax.rem(c + i, cols)), device_id_type=pl.DeviceIdType.MESH)
    pl.semaphore_wait(barrier, rows + cols - 2)

    factors, inverses = (one_ref, two_ref), (inv_one, inv_two)

    def prepare_products():
        inv_one_t[...] = inv_one[...].T
        inv_two_t[...] = inv_two[...].T
        mixed[...] = high(inv_two[...], link_ref[...])
        mixed_t[...] = mixed[...].T
        adj_one[...] = high(one_ref[...].T, adj_ref[0])
        adj_two[...] = high(two_ref[...].T, adj_ref[1])

    jobs = [lambda: place_tiles(factors, inverses), lambda: join_tiles(factors, inverses), prepare_products]

    panels = Spread(held, rows, send_panels, recv_panels)
    hop = panels.hop

    def add_group(step):
        panels.other_core(step)
        for away, there in panels.origins(step):
            z = panels.z + away

            @pl.when(there)
            def _():
                columns = pl.ds(pl.multiple_of(z * (hop * slab), hop * slab), hop * slab)
                block = held[pl.ds(z * hop, hop)].reshape(hop * slab, 2 * width)
                term = -2.0 * high(matrix[:, columns], block)
                if step == 0:
                    total[...] = term
                else:
                    total[...] += term

    panels.begin()
    for step in range(1, panels.depth):
        if jobs:
            jobs.pop(0)()
        panels.along(step)
        panels.across(step - 1)
        add_group(step - 1)
    for job in jobs:
        job()
    panels.across(panels.depth - 1)
    add_group(panels.depth - 1)

    mesh_id = lambda i: lax.rem(c + i, cols)
    for i in range(1, cols):
        peer = mesh_id(i)
        to_peer(
            total.at[pl.ds(peer * slab, slab)], landed.at[c], send_carried.at[peer], recv_carried.at[c], (r, peer)
        ).start()
    carried = total[pl.ds(c * slab, slab)]
    for i in range(1, cols):
        peer = mesh_id(i)
        to_peer(
            total.at[pl.ds(peer * slab, slab)], landed.at[peer], send_carried.at[peer], recv_carried.at[peer], (r, peer)
        ).wait_recv()
        carried = carried + landed[peer]
    pressed[:, pl.ds(0, width)] = up_one[...] + carried[:, :width]
    pressed[:, pl.ds(width, width)] = up_two[...] + carried[:, width:]

    flipped_one = pressed[:, pl.ds(0, width)].T
    flipped_two = pressed[:, pl.ds(width, width)].T
    outgoing[:, pl.ds(0, share)] = flipped_one.reshape(rows, share, slab)
    outgoing[:, pl.ds(share, share)] = flipped_two.reshape(rows, share, slab)

    def slice_copy(peer, origin):
        return to_peer(
            outgoing.at[peer], incoming.at[origin], send_slices.at[peer], recv_slices.at[origin], (peer, c)
        )

    @pl.loop(1, rows)
    def _(i):
        slice_copy(lax.rem(r + i, rows), r).start()

    incoming[r] = outgoing[r]
    found_two = high(pressed[:, pl.ds(width, width)], inv_two[...])
    grad_two[...] = found_two
    grad_one[...] = high(pressed[:, pl.ds(0, width)] - high(found_two, link_ref[...]), inv_one[...])

    @pl.loop(1, rows)
    def _(i):
        peer = lax.rem(r + i, rows)
        slice_copy(peer, peer).wait_recv()

    per = TILE // slab
    for t in range(rows // per):
        turned[:, pl.ds(t * TILE, TILE)] = jnp.concatenate([incoming[t * per + i] for i in range(per)], axis=1)
    found = high(turned[...], held[...].reshape(rows * slab, 2 * width))
    part[0] = found[:share, :width]
    part[1] = found[share:, :width]
    part[2] = found[share:, width:]
    for i in range(1, cols):
        peer = mesh_id(i)
        to_peer(part, parts.at[c], send_part.at[peer], recv_part.at[c], (r, peer)).start()
    summed = part[...]
    for i in range(1, cols):
        peer = mesh_id(i)
        to_peer(part, parts.at[peer], send_part.at[peer], recv_part.at[peer], (r, peer)).wait_recv()
    for i in range(cols):
        @pl.when(c == i)
        def _():
            parts[i] = part[...]

    summed = parts[0]
    for i in range(1, cols):
        summed = summed + parts[i]
    sums[r] = summed

    whole_sums = Spread(sums, rows, send_sums, recv_sums)
    whole_sums.begin()
    for step in range(1, whole_sums.depth):
        whole_sums.along(step)
        whole_sums.across(step - 1)
    whole_sums.across(whole_sums.depth - 1)
    for step in range(whole_sums.depth):
        whole_sums.other_core(step)

    panels.end()
    whole_sums.end()
    for i in range(1, cols):
        peer = mesh_id(i)
        to_peer(
            total.at[pl.ds(peer * slab, slab)], landed.at[peer], send_carried.at[peer], recv_carried.at[peer], (r, peer)
        ).wait_send()
        to_peer(part, parts.at[peer], send_part.at[peer], recv_part.at[peer], (r, peer)).wait_send()

    @pl.loop(1, rows)
    def _(i):
        peer = lax.rem(r + i, rows)
        slice_copy(peer, peer).wait_send()


def finish_blocks(sums, *rest):
    width = sums.shape[3]
    finish([sums[:, i].reshape(width, width) for i in range(3)], *rest)


def whole(count):
    return [pl.BlockSpec(memory_space=pltpu.VMEM)] * count


def local(
    rows,
    cols,
    trail_adjoint,
    panel_one,
    panel_two,
    upstream_one,
    upstream_two,
    pivot_one,
    pivot_two,
    link_block,
    pivot_adjoint,
):
    slab, width = panel_one.shape
    share = width // rows
    matrix = trail_adjoint.reshape(trail_adjoint.shape[1], trail_adjoint.shape[3])
    float_of = lambda *shape: jax.ShapeDtypeStruct(shape, jnp.float32)
    vmem = lambda *shape: pltpu.VMEM(shape, jnp.float32)
    dma = lambda *shape: pltpu.SemaphoreType.DMA(shape)
    square = float_of(width, width)
    strip = float_of(slab, width)
    cost = pl.CostEstimate(flops=16 * width**3, bytes_accessed=48 * width**2, transcendentals=0)
    found = pl.pallas_call(
        functools.partial(sweep, rows, cols),
        out_shape=[strip, strip, float_of(rows, 3, share, width)] + [square] * 8,
        in_specs=whole(9),
        out_specs=whole(11),
        scratch_shapes=[
            vmem(rows, slab, 2 * width),
            vmem(cols * slab, 2 * width),
            vmem(cols, slab, 2 * width),
            vmem(slab, 2 * width),
            vmem(rows, 2 * share, slab),
            vmem(rows, 2 * share, slab),
            vmem(2 * share, rows * slab),
            vmem(3, share, width),
            vmem(cols, 3, share, width),
            dma(4, rows),
            dma(rows),
            dma(cols),
            dma(cols),
            dma(rows),
            dma(rows),
            dma(cols),
            dma(cols),
            dma(4, rows),
            dma(rows),
        ],
        compiler_params=pltpu.CompilerParams(
            collective_id=0, has_side_effects=True, vmem_limit_bytes=56 << 20
        ),
        cost_estimate=cost,
        name="sweep",
    )(
        matrix,
        panel_one,
        panel_two,
        upstream_one,
        upstream_two,
        pivot_one,
        pivot_two,
        link_block,
        pivot_adjoint,
    )
    grad_one, grad_two = found[:2]
    grads = pl.pallas_call(
        finish_blocks,
        out_shape=float_of(3, width, width),
        in_specs=whole(9),
        out_specs=pl.BlockSpec(memory_space=pltpu.VMEM),
        compiler_params=pltpu.CompilerParams(vmem_limit_bytes=48 << 20),
        cost_estimate=cost,
        name="finish",
    )(*found[2:])
    return grad_one, grad_two, grads


def solution(mesh):
    return jax.shard_map(
        functools.partial(local, mesh.shape["row"], mesh.shape["col"]),
        mesh=mesh,
        in_specs=(
            P("row", None, "col", None),
            P(("row", "col"), None),
            P(("row", "col"), None),
            P(("row", "col"), None),
            P(("row", "col"), None),
            P(),
            P(),
            P(),
            P(),
        ),
        out_specs=(P(("row", "col"), None), P(("row", "col"), None), P()),
        check_vma=False,
    )
```

```python
import functools

import jax
import jax.numpy as jnp
from jax import lax
from jax.experimental import pallas as pl
from jax.experimental.pallas import tpu as pltpu
from jax.sharding import PartitionSpec as P

TILE = 128
BASE = 8
CORES = 2
SIDE = 2


def dot(left, right, precision=lax.Precision.HIGHEST):
    return jnp.dot(left, right, precision=precision, preferred_element_type=jnp.float32)


def high(left, right):
    return dot(left, right, lax.Precision.HIGH)


def tile_inverses(tiles):
    size = tiles[0].shape[0]
    row = lax.broadcasted_iota(jnp.int32, (size, size), 0)
    col = lax.broadcasted_iota(jnp.int32, (size, size), 1)
    eye = row == col
    one = jnp.where(eye, 1.0, 0.0)
    base = (row // BASE == col // BASE) & (row > col)
    nil, across = [], []
    for tile in tiles:
        diag = jnp.where(eye, tile, 0.0)
        down = 1.0 / jnp.sum(diag, axis=1, keepdims=True)
        across.append(1.0 / jnp.sum(diag, axis=0, keepdims=True))
        nil.append(jnp.where(base, -tile * down, 0.0))
    found = [one + n for n in nil]
    power = nil
    reach = 2
    while reach < BASE:
        power = [dot(p, p) for p in power]
        found = [f + dot(f, p) for f, p in zip(found, power)]
        reach *= 2
    found = [f * a for f, a in zip(found, across)]
    step = BASE
    while step < size:
        level = (row // (2 * step) == col // (2 * step)) & (row // step != col // step) & (row > col)
        below = [dot(jnp.where(level, t, 0.0), f) for t, f in zip(tiles, found)]
        found = [f - dot(f, b) for f, b in zip(found, below)]
        step *= 2
    return found


def place_tiles(factors, outs):
    width = factors[0].shape[0]
    count = width // TILE
    spans = [pl.ds(t * TILE, TILE) for t in range(count)]
    found = tile_inverses([f[s, s] for f in factors for s in spans])
    for i, out in enumerate(outs):
        out[...] = jnp.zeros_like(out)
        for t, s in enumerate(spans):
            out[s, s] = found[i * count + t]


def join_tiles(factors, outs):
    width = factors[0].shape[0]
    step = TILE
    while step < width:
        for at in range(0, width, 2 * step):
            top, low = pl.ds(at, step), pl.ds(at + step, step)
            belows = [dot(f[low, top], o[top, top]) for f, o in zip(factors, outs)]
            for o, b in zip(outs, belows):
                o[low, top] = -dot(o[low, low], b)
        step *= 2


def half_symmetric(x):
    row = lax.broadcasted_iota(jnp.int32, x.shape, 0)
    col = lax.broadcasted_iota(jnp.int32, x.shape, 1)
    return 0.5 * (jnp.where(row > col, x, 0.0) + jnp.where(row >= col, x, 0.0).T)


def times_lower(left, lower):
    half = lower.shape[0] // 2
    return jnp.concatenate(
        [high(left, lower[:, pl.ds(0, half)]), high(left[:, half:], lower[pl.ds(half, half), pl.ds(half, half)])],
        axis=1,
    )


def upper_times(upper, right):
    half = upper.shape[0] // 2
    return jnp.concatenate(
        [high(upper[pl.ds(0, half)], right), high(upper[pl.ds(half, half), pl.ds(half, half)], right[half:])],
        axis=0,
    )


def finish(sum_one, sum_link, sum_two, inv_one, inv_two, inv_one_t, inv_two_t, mixed, mixed_t, adj_one, adj_two, out):
    sym_two = half_symmetric(adj_two[...] - sum_two[...])
    out[2] = upper_times(inv_two_t, times_lower(sym_two, inv_two))
    turned = high(sym_two, mixed[...])
    link = sum_link[...]
    out[1] = -times_lower(upper_times(inv_two_t, link + 2.0 * turned), inv_one)
    cross = high(mixed_t[...], link + turned)
    sym_one = half_symmetric(adj_one[...] - sum_one[...]) + 0.5 * (cross + cross.T)
    out[0] = upper_times(inv_one_t, times_lower(sym_one, inv_one))


class Spread:
    def __init__(self, buf, rows, send, recv):
        self.buf, self.send, self.recv = buf, send, recv
        self.r, self.c = lax.axis_index("row"), lax.axis_index("col")
        self.depth = rows // (SIDE * CORES)
        self.z = self.r // (SIDE * CORES)
        core, side = self.r % CORES, self.r // CORES % SIDE
        self.core_peer = self.r + 1 - 2 * core
        self.side_peer = self.r + CORES - 2 * CORES * side
        self.hop = SIDE * CORES
        self.sent = []

    def copy(self, block, way, target):
        return pltpu.make_async_remote_copy(
            src_ref=self.buf.at[block],
            dst_ref=self.buf.at[block],
            send_sem=self.send.at[way, block],
            recv_sem=self.recv.at[block],
            device_id=(target, self.c),
            device_id_type=pl.DeviceIdType.MESH,
        )

    def pass_on(self, block, way, target, when):
        @pl.when(when)
        def _():
            self.copy(block, way, target).start()

        self.sent.append((block, way, target, when))

    def await_block(self, block, when):
        @pl.when(when)
        def _():
            self.copy(block, 0, self.core_peer).wait_recv()

    def begin(self):
        r, z = self.r, self.z
        self.pass_on(r, 0, r + self.hop, z < self.depth - 1)
        self.pass_on(r, 1, r - self.hop, z > 0)
        self.pass_on(r, 2, self.side_peer, z >= 0)
        self.pass_on(r, 3, self.core_peer, z >= 0)

    def origins(self, step):
        if step == 0:
            return [(0, self.z >= 0)]
        return [(-step, self.z >= step), (step, self.z < self.depth - step)]

    def along(self, step):
        z, hop = self.z, self.hop
        for away, there in self.origins(step):
            block = self.r + away * hop
            self.await_block(block, there)
            if away < 0:
                self.pass_on(block, 0, self.r + hop, there & (z < self.depth - 1))
            else:
                self.pass_on(block, 1, self.r - hop, there & (z > 0))
            self.pass_on(block, 2, self.side_peer, there)
            self.pass_on(block, 3, self.core_peer, there)

    def across(self, step):
        for away, there in self.origins(step):
            block = self.side_peer + away * self.hop
            self.await_block(block, there)
            self.pass_on(block, 3, self.core_peer, there)

    def other_core(self, step):
        for away, there in self.origins(step):
            self.await_block(self.core_peer + away * self.hop, there)
            flipped = self.side_peer + self.core_peer - self.r
            self.await_block(flipped + away * self.hop, there)

    def end(self):
        for block, way, target, when in self.sent:
            @pl.when(when)
            def _():
                self.copy(block, way, target).wait_send()


def to_peer(src, dst, send, recv, target):
    return pltpu.make_async_remote_copy(
        src_ref=src,
        dst_ref=dst,
        send_sem=send,
        recv_sem=recv,
        device_id=target,
        device_id_type=pl.DeviceIdType.MESH,
    )


def sweep(
    rows,
    cols,
    matrix_in,
    panel_one,
    panel_two,
    up_one_in,
    up_two_in,
    one_in,
    two_in,
    link_in,
    adj_in,
    grad_one,
    grad_two,
    grads,
    matrix,
    up_one,
    up_two,
    one_ref,
    two_ref,
    link_ref,
    adj_ref,
    read_sem,
    sums,
    sum_one,
    sum_link,
    sum_two,
    inv_one,
    inv_two,
    inv_one_t,
    inv_two_t,
    mixed,
    mixed_t,
    adj_one,
    adj_two,
    held,
    total,
    landed,
    pressed,
    outgoing,
    incoming,
    turned,
    part,
    parts,
    send_panels,
    recv_panels,
    send_carried,
    recv_carried,
    send_slices,
    recv_slices,
    send_part,
    recv_part,
    send_sums,
    recv_sums,
):
    r, c = lax.axis_index("row"), lax.axis_index("col")
    slab, width = panel_one.shape
    share = width // rows
    reads = [
        pltpu.make_async_copy(source, target, read_sem.at[i])
        for i, (source, target) in enumerate(
            [
                (one_in, one_ref),
                (two_in, two_ref),
                (link_in, link_ref),
                (adj_in, adj_ref),
                (matrix_in.at[0, :, 0], matrix),
                (up_one_in, up_one),
                (up_two_in, up_two),
            ]
        )
    ]
    held[r, :, pl.ds(0, width)] = panel_one[...]
    held[r, :, pl.ds(width, width)] = panel_two[...]

    barrier = pltpu.get_barrier_semaphore()

    @pl.loop(1, rows)
    def _(i):
        pl.semaphore_signal(barrier, inc=1, device_id=(lax.rem(r + i, rows), c), device_id_type=pl.DeviceIdType.MESH)

    for i in range(1, cols):
        pl.semaphore_signal(barrier, inc=1, device_id=(r, lax.rem(c + i, cols)), device_id_type=pl.DeviceIdType.MESH)
    pl.semaphore_wait(barrier, rows + cols - 2)

    factors, inverses = (one_ref, two_ref), (inv_one, inv_two)

    def prepare_products():
        inv_one_t[...] = inv_one[...].T
        inv_two_t[...] = inv_two[...].T
        mixed[...] = high(inv_two[...], link_ref[...])
        mixed_t[...] = mixed[...].T
        adj_one[...] = high(one_ref[...].T, adj_ref[0])
        adj_two[...] = high(two_ref[...].T, adj_ref[1])

    jobs = [lambda: place_tiles(factors, inverses), lambda: join_tiles(factors, inverses), prepare_products]

    panels = Spread(held, rows, send_panels, recv_panels)
    hop = panels.hop

    def add_group(step):
        panels.other_core(step)
        for away, there in panels.origins(step):
            z = panels.z + away

            @pl.when(there)
            def _():
                columns = pl.ds(pl.multiple_of(z * (hop * slab), hop * slab), hop * slab)
                block = held[pl.ds(z * hop, hop)].reshape(hop * slab, 2 * width)
                term = -2.0 * high(matrix[:, columns], block)
                if step == 0:
                    total[...] = term
                else:
                    total[...] += term

    panels.begin()
    for read in reads:
        read.start()
    for read in reads:
        read.wait()
    for step in range(1, panels.depth):
        if jobs:
            jobs.pop(0)()
        panels.along(step)
        panels.across(step - 1)
        add_group(step - 1)
    for job in jobs:
        job()
    panels.across(panels.depth - 1)
    add_group(panels.depth - 1)

    mesh_id = lambda i: lax.rem(c + i, cols)
    for i in range(1, cols):
        peer = mesh_id(i)
        to_peer(
            total.at[pl.ds(peer * slab, slab)], landed.at[c], send_carried.at[peer], recv_carried.at[c], (r, peer)
        ).start()
    carried = total[pl.ds(c * slab, slab)]
    for i in range(1, cols):
        peer = mesh_id(i)
        to_peer(
            total.at[pl.ds(peer * slab, slab)], landed.at[peer], send_carried.at[peer], recv_carried.at[peer], (r, peer)
        ).wait_recv()
        carried = carried + landed[peer]
    pressed[:, pl.ds(0, width)] = up_one[...] + carried[:, :width]
    pressed[:, pl.ds(width, width)] = up_two[...] + carried[:, width:]

    flipped_one = pressed[:, pl.ds(0, width)].T
    flipped_two = pressed[:, pl.ds(width, width)].T
    for i in range(rows):
        mirror = rows - 1 - i
        outgoing[i] = jnp.concatenate(
            [flipped_one[i * share : (i + 1) * share], flipped_two[mirror * share : (mirror + 1) * share]], axis=1
        )

    def slice_copy(peer, origin):
        return to_peer(
            outgoing.at[peer], incoming.at[origin], send_slices.at[peer], recv_slices.at[origin], (peer, c)
        )

    @pl.loop(1, rows)
    def _(i):
        slice_copy(lax.rem(r + i, rows), r).start()

    incoming[r] = outgoing[r]
    found_two = high(pressed[:, pl.ds(width, width)], inv_two[...])
    grad_two[...] = found_two
    grad_one[...] = high(pressed[:, pl.ds(0, width)] - high(found_two, link_ref[...]), inv_one[...])

    @pl.loop(1, rows)
    def _(i):
        peer = lax.rem(r + i, rows)
        slice_copy(peer, peer).wait_recv()

    per = TILE // slab
    for t in range(rows // per):
        pieces = [incoming[t * per + i] for i in range(per)]
        turned[pl.ds(0, share), pl.ds(t * TILE, TILE)] = jnp.concatenate([p[:, :slab] for p in pieces], axis=1)
        turned[pl.ds(share, share), pl.ds(t * TILE, TILE)] = jnp.concatenate([p[:, slab:] for p in pieces], axis=1)
    found = high(turned[...], held[...].reshape(rows * slab, 2 * width))
    part[:, pl.ds(0, width)] = found[share:, :width]
    levels = width // TILE
    for level in range(levels):

        @pl.when(r * share // TILE == level)
        def _():
            reach = (level + 1) * TILE
            part[:, pl.ds(width, reach)] = found[:share, :reach]
            part[:, pl.ds(width + reach, width + TILE - reach)] = found[share:, width : 2 * width + TILE - reach]

    for i in range(1, cols):
        peer = mesh_id(i)
        to_peer(part, parts.at[c], send_part.at[peer], recv_part.at[c], (r, peer)).start()
    parts[c] = part[...]
    for i in range(1, cols):
        peer = mesh_id(i)
        to_peer(part, parts.at[peer], send_part.at[peer], recv_part.at[peer], (r, peer)).wait_recv()
    summed = parts[0]
    for i in range(1, cols):
        summed = summed + parts[i]
    sums[r] = summed

    whole_sums = Spread(sums, rows, send_sums, recv_sums)
    whole_sums.begin()
    for step in range(1, whole_sums.depth):
        whole_sums.along(step)
        whole_sums.across(step - 1)
    whole_sums.across(whole_sums.depth - 1)
    for step in range(whole_sums.depth):
        whole_sums.other_core(step)
    sum_one[...] = jnp.zeros_like(sum_one)
    sum_two[...] = jnp.zeros_like(sum_two)
    for i in range(rows):
        reach = (i * share // TILE + 1) * TILE
        own, mirror = pl.ds(i * share, share), pl.ds((rows - 1 - i) * share, share)
        sum_link[mirror] = sums[i, :, pl.ds(0, width)]
        sum_one[own, pl.ds(0, reach)] = sums[i, :, pl.ds(width, reach)]
        sum_two[mirror, pl.ds(0, width + TILE - reach)] = sums[i, :, pl.ds(width + reach, width + TILE - reach)]
    finish(
        sum_one, sum_link, sum_two, inv_one, inv_two, inv_one_t, inv_two_t, mixed, mixed_t, adj_one, adj_two, grads
    )

    panels.end()
    whole_sums.end()
    for i in range(1, cols):
        peer = mesh_id(i)
        to_peer(
            total.at[pl.ds(peer * slab, slab)], landed.at[peer], send_carried.at[peer], recv_carried.at[peer], (r, peer)
        ).wait_send()
        to_peer(part, parts.at[peer], send_part.at[peer], recv_part.at[peer], (r, peer)).wait_send()

    @pl.loop(1, rows)
    def _(i):
        peer = lax.rem(r + i, rows)
        slice_copy(peer, peer).wait_send()


def whole(count):
    return [pl.BlockSpec(memory_space=pltpu.VMEM)] * count


def local(
    rows,
    cols,
    trail_adjoint,
    panel_one,
    panel_two,
    upstream_one,
    upstream_two,
    pivot_one,
    pivot_two,
    link_block,
    pivot_adjoint,
):
    slab, width = panel_one.shape
    share = width // rows
    float_of = lambda *shape: jax.ShapeDtypeStruct(shape, jnp.float32)
    vmem = lambda *shape: pltpu.VMEM(shape, jnp.float32)
    dma = lambda *shape: pltpu.SemaphoreType.DMA(shape)
    square = vmem(width, width)
    strip = float_of(slab, width)
    cost = pl.CostEstimate(flops=16 * width**3, bytes_accessed=48 * width**2, transcendentals=0)
    packed = 2 * width + TILE
    return pl.pallas_call(
        functools.partial(sweep, rows, cols),
        out_shape=[strip, strip, float_of(3, width, width)],
        in_specs=[pl.BlockSpec(memory_space=pl.ANY)] + whole(2) + [pl.BlockSpec(memory_space=pl.ANY)] * 6,
        out_specs=whole(3),
        scratch_shapes=[
            vmem(cols * slab, rows * slab),
            vmem(slab, width),
            vmem(slab, width),
            square,
            square,
            square,
            vmem(2, width, width),
            dma(7),
            vmem(rows, share, packed),
        ]
        + [square] * 11
        + [
            vmem(rows, slab, 2 * width),
            vmem(cols * slab, 2 * width),
            vmem(cols, slab, 2 * width),
            vmem(slab, 2 * width),
            vmem(rows, share, 2 * slab),
            vmem(rows, share, 2 * slab),
            vmem(2 * share, rows * slab),
            vmem(share, packed),
            vmem(cols, share, packed),
            dma(4, rows),
            dma(rows),
            dma(cols),
            dma(cols),
            dma(rows),
            dma(rows),
            dma(cols),
            dma(cols),
            dma(4, rows),
            dma(rows),
        ],
        compiler_params=pltpu.CompilerParams(
            collective_id=0, has_side_effects=True, vmem_limit_bytes=56 << 20
        ),
        cost_estimate=cost,
        name="sweep",
    )(
        trail_adjoint,
        panel_one,
        panel_two,
        upstream_one,
        upstream_two,
        pivot_one,
        pivot_two,
        link_block,
        pivot_adjoint,
    )


def solution(mesh):
    return jax.shard_map(
        functools.partial(local, mesh.shape["row"], mesh.shape["col"]),
        mesh=mesh,
        in_specs=(
            P("row", None, "col", None),
            P(("row", "col"), None),
            P(("row", "col"), None),
            P(("row", "col"), None),
            P(("row", "col"), None),
            P(),
            P(),
            P(),
            P(),
        ),
        out_specs=(P(("row", "col"), None), P(("row", "col"), None), P()),
        check_vma=False,
    )
```

```python
import functools

import jax
import jax.numpy as jnp
from jax import lax
from jax.experimental import pallas as pl
from jax.experimental.pallas import tpu as pltpu
from jax.sharding import PartitionSpec as P

TILE = 128
BASE = 8
CORES = 2
SIDE = 2


def dot(left, right, precision=lax.Precision.HIGHEST):
    return jnp.dot(left, right, precision=precision, preferred_element_type=jnp.float32)


def high(left, right):
    return dot(left, right, lax.Precision.HIGH)


def tile_grid(size):
    return lax.broadcasted_iota(jnp.int32, (size, size), 0), lax.broadcasted_iota(jnp.int32, (size, size), 1)


def base_inverses(tiles):
    row, col = tile_grid(tiles[0].shape[0])
    eye = row == col
    one = jnp.where(eye, 1.0, 0.0)
    base = (row // BASE == col // BASE) & (row > col)
    nil, across = [], []
    for tile in tiles:
        diag = jnp.where(eye, tile, 0.0)
        down = 1.0 / jnp.sum(diag, axis=1, keepdims=True)
        across.append(1.0 / jnp.sum(diag, axis=0, keepdims=True))
        nil.append(jnp.where(base, -tile * down, 0.0))
    found = [one + n for n in nil]
    power = nil
    reach = 2
    while reach < BASE:
        power = [dot(p, p) for p in power]
        found = [f + dot(f, p) for f, p in zip(found, power)]
        reach *= 2
    return [f * a for f, a in zip(found, across)]


def raise_inverses(tiles, found, step, last):
    row, col = tile_grid(tiles[0].shape[0])
    while step < last:
        level = (row // (2 * step) == col // (2 * step)) & (row // step != col // step) & (row > col)
        below = [dot(jnp.where(level, t, 0.0), f) for t, f in zip(tiles, found)]
        found = [f - dot(f, b) for f, b in zip(found, below)]
        step *= 2
    return found


def tile_spans(factors):
    spans = [pl.ds(t * TILE, TILE) for t in range(factors[0].shape[0] // TILE)]
    return [(i, s) for i in range(len(factors)) for s in spans]


def place_bases(factors, outs):
    spans = tile_spans(factors)
    found = base_inverses([factors[i][s, s] for i, s in spans])
    for out in outs:
        out[...] = jnp.zeros_like(out)
    for (i, s), f in zip(spans, found):
        outs[i][s, s] = f


def raise_tiles(factors, outs, step, last):
    spans = tile_spans(factors)
    found = raise_inverses([factors[i][s, s] for i, s in spans], [outs[i][s, s] for i, s in spans], step, last)
    for (i, s), f in zip(spans, found):
        outs[i][s, s] = f


def join_tiles(factors, outs):
    width = factors[0].shape[0]
    step = TILE
    while step < width:
        for at in range(0, width, 2 * step):
            top, low = pl.ds(at, step), pl.ds(at + step, step)
            belows = [dot(f[low, top], o[top, top]) for f, o in zip(factors, outs)]
            for o, b in zip(outs, belows):
                o[low, top] = -dot(o[low, low], b)
        step *= 2


def half_symmetric(x):
    row = lax.broadcasted_iota(jnp.int32, x.shape, 0)
    col = lax.broadcasted_iota(jnp.int32, x.shape, 1)
    return 0.5 * (jnp.where(row > col, x, 0.0) + jnp.where(row >= col, x, 0.0).T)


def times_lower(left, lower):
    half = lower.shape[0] // 2
    return jnp.concatenate(
        [high(left, lower[:, pl.ds(0, half)]), high(left[:, half:], lower[pl.ds(half, half), pl.ds(half, half)])],
        axis=1,
    )


def upper_times(upper, right):
    half = upper.shape[0] // 2
    return jnp.concatenate(
        [high(upper[pl.ds(0, half)], right), high(upper[pl.ds(half, half), pl.ds(half, half)], right[half:])],
        axis=0,
    )


def finish(sum_one, sum_link, sum_two, inv_one, inv_two, inv_one_t, inv_two_t, mixed, mixed_t, adj_one, adj_two, out, writes):
    sym_two = half_symmetric(adj_two[...] - sum_two[...])
    out[2] = upper_times(inv_two_t, times_lower(sym_two, inv_two))
    writes[2].start()
    turned = high(sym_two, mixed[...])
    link = sum_link[...]
    out[1] = -times_lower(upper_times(inv_two_t, link + 2.0 * turned), inv_one)
    writes[1].start()
    cross = high(mixed_t[...], link + turned)
    sym_one = half_symmetric(adj_one[...] - sum_one[...]) + 0.5 * (cross + cross.T)
    out[0] = upper_times(inv_one_t, times_lower(sym_one, inv_one))
    writes[0].start()


class Spread:
    def __init__(self, buf, rows, send, recv):
        self.buf, self.send, self.recv = buf, send, recv
        self.r, self.c = lax.axis_index("row"), lax.axis_index("col")
        self.depth = rows // (SIDE * CORES)
        self.z = self.r // (SIDE * CORES)
        core, side = self.r % CORES, self.r // CORES % SIDE
        self.core_peer = self.r + 1 - 2 * core
        self.side_peer = self.r + CORES - 2 * CORES * side
        self.hop = SIDE * CORES
        self.sent = []

    def copy(self, block, way, target):
        return pltpu.make_async_remote_copy(
            src_ref=self.buf.at[block],
            dst_ref=self.buf.at[block],
            send_sem=self.send.at[way, block],
            recv_sem=self.recv.at[block],
            device_id=(target, self.c),
            device_id_type=pl.DeviceIdType.MESH,
        )

    def pass_on(self, block, way, target, when):
        @pl.when(when)
        def _():
            self.copy(block, way, target).start()

        self.sent.append((block, way, target, when))

    def await_block(self, block, when):
        @pl.when(when)
        def _():
            self.copy(block, 0, self.core_peer).wait_recv()

    def begin(self):
        r, z = self.r, self.z
        self.pass_on(r, 0, r + self.hop, z < self.depth - 1)
        self.pass_on(r, 1, r - self.hop, z > 0)
        self.pass_on(r, 2, self.side_peer, z >= 0)
        self.pass_on(r, 3, self.core_peer, z >= 0)

    def origins(self, step):
        if step == 0:
            return [(0, self.z >= 0)]
        return [(-step, self.z >= step), (step, self.z < self.depth - step)]

    def along(self, step):
        z, hop = self.z, self.hop
        for away, there in self.origins(step):
            block = self.r + away * hop
            self.await_block(block, there)
            if away < 0:
                self.pass_on(block, 0, self.r + hop, there & (z < self.depth - 1))
            else:
                self.pass_on(block, 1, self.r - hop, there & (z > 0))
            self.pass_on(block, 2, self.side_peer, there)
            self.pass_on(block, 3, self.core_peer, there)

    def across(self, step):
        for away, there in self.origins(step):
            block = self.side_peer + away * self.hop
            self.await_block(block, there)
            self.pass_on(block, 3, self.core_peer, there)

    def other_core(self, step):
        for away, there in self.origins(step):
            self.await_block(self.core_peer + away * self.hop, there)
            flipped = self.side_peer + self.core_peer - self.r
            self.await_block(flipped + away * self.hop, there)

    def end(self):
        for block, way, target, when in self.sent:
            @pl.when(when)
            def _():
                self.copy(block, way, target).wait_send()


def to_peer(src, dst, send, recv, target):
    return pltpu.make_async_remote_copy(
        src_ref=src,
        dst_ref=dst,
        send_sem=send,
        recv_sem=recv,
        device_id=target,
        device_id_type=pl.DeviceIdType.MESH,
    )


def sweep(
    rows,
    cols,
    matrix_in,
    panel_one,
    panel_two,
    up_one_in,
    up_two_in,
    one_in,
    two_in,
    link_in,
    adj_in,
    grad_one_out,
    grad_two_out,
    grads_out,
    grad_one,
    grad_two,
    grads,
    write_sem,
    matrix,
    up_one,
    up_two,
    one_ref,
    two_ref,
    link_ref,
    adj_ref,
    read_sem,
    sums,
    sum_one,
    sum_link,
    sum_two,
    inv_one,
    inv_two,
    inv_one_t,
    inv_two_t,
    mixed,
    mixed_t,
    adj_one,
    adj_two,
    held,
    total,
    landed,
    pressed,
    outgoing,
    incoming,
    turned,
    part,
    parts,
    send_panels,
    recv_panels,
    send_carried,
    recv_carried,
    send_slices,
    recv_slices,
    send_part,
    recv_part,
    send_sums,
    recv_sums,
):
    r, c = lax.axis_index("row"), lax.axis_index("col")
    slab, width = panel_one.shape
    share = width // rows
    reads = [
        pltpu.make_async_copy(source, target, read_sem.at[i])
        for i, (source, target) in enumerate(
            [
                (one_in, one_ref),
                (two_in, two_ref),
                (matrix_in.at[0, :, 0], matrix),
                (link_in, link_ref),
                (adj_in, adj_ref),
                (up_one_in, up_one),
                (up_two_in, up_two),
            ]
        )
    ]
    held[r, :, pl.ds(0, width)] = panel_one[...]
    held[r, :, pl.ds(width, width)] = panel_two[...]

    barrier = pltpu.get_barrier_semaphore()

    @pl.loop(1, rows)
    def _(i):
        pl.semaphore_signal(barrier, inc=1, device_id=(lax.rem(r + i, rows), c), device_id_type=pl.DeviceIdType.MESH)

    for i in range(1, cols):
        pl.semaphore_signal(barrier, inc=1, device_id=(r, lax.rem(c + i, cols)), device_id_type=pl.DeviceIdType.MESH)
    pl.semaphore_wait(barrier, rows + cols - 2)

    factors, inverses = (one_ref, two_ref), (inv_one, inv_two)

    def first_job():
        for read in reads[:3]:
            read.wait()
        place_bases(factors, inverses)

    def second_job():
        raise_tiles(factors, inverses, BASE, TILE)
        for read in reads[3:]:
            read.wait()

    def third_job():
        join_tiles(factors, inverses)
        inv_one_t[...] = inv_one[...].T
        inv_two_t[...] = inv_two[...].T

    def fourth_job():
        mixed[...] = high(inv_two[...], link_ref[...])
        mixed_t[...] = mixed[...].T
        adj_one[...] = high(one_ref[...].T, adj_ref[0])
        adj_two[...] = high(two_ref[...].T, adj_ref[1])

    jobs = [first_job, second_job, third_job, fourth_job]

    panels = Spread(held, rows, send_panels, recv_panels)
    hop = panels.hop

    def add_group(step):
        panels.other_core(step)
        for away, there in panels.origins(step):
            z = panels.z + away

            @pl.when(there)
            def _():
                columns = pl.ds(pl.multiple_of(z * (hop * slab), hop * slab), hop * slab)
                block = held[pl.ds(z * hop, hop)].reshape(hop * slab, 2 * width)
                term = -2.0 * high(matrix[:, columns], block)
                if step == 0:
                    total[...] = term
                else:
                    total[...] += term

    panels.begin()
    for read in reads:
        read.start()
    for step in range(1, panels.depth):
        if jobs:
            jobs.pop(0)()
        panels.along(step)
        panels.across(step - 1)
        add_group(step - 1)
    for job in jobs:
        job()
    panels.across(panels.depth - 1)
    add_group(panels.depth - 1)

    mesh_id = lambda i: lax.rem(c + i, cols)
    for i in range(1, cols):
        peer = mesh_id(i)
        to_peer(
            total.at[pl.ds(peer * slab, slab)], landed.at[c], send_carried.at[peer], recv_carried.at[c], (r, peer)
        ).start()
    carried = total[pl.ds(c * slab, slab)]
    for i in range(1, cols):
        peer = mesh_id(i)
        to_peer(
            total.at[pl.ds(peer * slab, slab)], landed.at[peer], send_carried.at[peer], recv_carried.at[peer], (r, peer)
        ).wait_recv()
        carried = carried + landed[peer]
    pressed[:, pl.ds(0, width)] = up_one[...] + carried[:, :width]
    pressed[:, pl.ds(width, width)] = up_two[...] + carried[:, width:]

    flipped_one = pressed[:, pl.ds(0, width)].T
    flipped_two = pressed[:, pl.ds(width, width)].T
    for i in range(rows):
        mirror = rows - 1 - i
        outgoing[i] = jnp.concatenate(
            [flipped_one[i * share : (i + 1) * share], flipped_two[mirror * share : (mirror + 1) * share]], axis=1
        )

    def slice_copy(peer, origin):
        return to_peer(
            outgoing.at[peer], incoming.at[origin], send_slices.at[peer], recv_slices.at[origin], (peer, c)
        )

    @pl.loop(1, rows)
    def _(i):
        slice_copy(lax.rem(r + i, rows), r).start()

    writes = [
        pltpu.make_async_copy(source, target, write_sem.at[i])
        for i, (source, target) in enumerate(
            [(grads.at[k], grads_out.at[k]) for k in range(3)] + [(grad_one, grad_one_out), (grad_two, grad_two_out)]
        )
    ]
    incoming[r] = outgoing[r]
    found_two = high(pressed[:, pl.ds(width, width)], inv_two[...])
    grad_two[...] = found_two
    grad_one[...] = high(pressed[:, pl.ds(0, width)] - high(found_two, link_ref[...]), inv_one[...])
    writes[3].start()
    writes[4].start()

    @pl.loop(1, rows)
    def _(i):
        peer = lax.rem(r + i, rows)
        slice_copy(peer, peer).wait_recv()

    per = TILE // slab
    for t in range(rows // per):
        pieces = [incoming[t * per + i] for i in range(per)]
        turned[pl.ds(0, share), pl.ds(t * TILE, TILE)] = jnp.concatenate([p[:, :slab] for p in pieces], axis=1)
        turned[pl.ds(share, share), pl.ds(t * TILE, TILE)] = jnp.concatenate([p[:, slab:] for p in pieces], axis=1)
    found = high(turned[...], held[...].reshape(rows * slab, 2 * width))
    part[:, pl.ds(0, width)] = found[share:, :width]
    levels = width // TILE
    for level in range(levels):

        @pl.when(r * share // TILE == level)
        def _():
            reach = (level + 1) * TILE
            part[:, pl.ds(width, reach)] = found[:share, :reach]
            part[:, pl.ds(width + reach, width + TILE - reach)] = found[share:, width : 2 * width + TILE - reach]

    for i in range(1, cols):
        peer = mesh_id(i)
        to_peer(part, parts.at[c], send_part.at[peer], recv_part.at[c], (r, peer)).start()
    parts[c] = part[...]
    for i in range(1, cols):
        peer = mesh_id(i)
        to_peer(part, parts.at[peer], send_part.at[peer], recv_part.at[peer], (r, peer)).wait_recv()
    summed = parts[0]
    for i in range(1, cols):
        summed = summed + parts[i]
    sums[r] = summed

    whole_sums = Spread(sums, rows, send_sums, recv_sums)
    whole_sums.begin()
    for step in range(1, whole_sums.depth):
        whole_sums.along(step)
        whole_sums.across(step - 1)
    whole_sums.across(whole_sums.depth - 1)
    for step in range(whole_sums.depth):
        whole_sums.other_core(step)
    sum_one[...] = jnp.zeros_like(sum_one)
    sum_two[...] = jnp.zeros_like(sum_two)
    for i in range(rows):
        reach = (i * share // TILE + 1) * TILE
        own, mirror = pl.ds(i * share, share), pl.ds((rows - 1 - i) * share, share)
        sum_link[mirror] = sums[i, :, pl.ds(0, width)]
        sum_one[own, pl.ds(0, reach)] = sums[i, :, pl.ds(width, reach)]
        sum_two[mirror, pl.ds(0, width + TILE - reach)] = sums[i, :, pl.ds(width + reach, width + TILE - reach)]
    finish(
        sum_one,
        sum_link,
        sum_two,
        inv_one,
        inv_two,
        inv_one_t,
        inv_two_t,
        mixed,
        mixed_t,
        adj_one,
        adj_two,
        grads,
        writes,
    )

    panels.end()
    whole_sums.end()
    for i in range(1, cols):
        peer = mesh_id(i)
        to_peer(
            total.at[pl.ds(peer * slab, slab)], landed.at[peer], send_carried.at[peer], recv_carried.at[peer], (r, peer)
        ).wait_send()
        to_peer(part, parts.at[peer], send_part.at[peer], recv_part.at[peer], (r, peer)).wait_send()

    @pl.loop(1, rows)
    def _(i):
        peer = lax.rem(r + i, rows)
        slice_copy(peer, peer).wait_send()

    for write in writes:
        write.wait()


def hand_on(*refs):
    *ends, sem = refs
    count = len(ends) // 2
    pairs = []
    for source, target in zip(ends[:count], ends[count:]):
        if len(source.shape) == 3:
            pairs += [(source.at[k], target.at[k]) for k in range(source.shape[0])]
        else:
            pairs.append((source, target))
    copies = [pltpu.make_async_copy(source, target, sem.at[i]) for i, (source, target) in enumerate(pairs)]
    for copy in copies:
        copy.start()
    for copy in copies:
        copy.wait()


def whole(count):
    return [pl.BlockSpec(memory_space=pltpu.VMEM)] * count


def local(
    rows,
    cols,
    trail_adjoint,
    panel_one,
    panel_two,
    upstream_one,
    upstream_two,
    pivot_one,
    pivot_two,
    link_block,
    pivot_adjoint,
):
    slab, width = panel_one.shape
    share = width // rows
    float_of = lambda *shape: jax.ShapeDtypeStruct(shape, jnp.float32)
    vmem = lambda *shape: pltpu.VMEM(shape, jnp.float32)
    dma = lambda *shape: pltpu.SemaphoreType.DMA(shape)
    square = vmem(width, width)
    strip = float_of(slab, width)
    cost = pl.CostEstimate(flops=16 * width**3, bytes_accessed=48 * width**2, transcendentals=0)
    packed = 2 * width + TILE
    results = [strip, strip, float_of(3, width, width)]
    anywhere = lambda count: [pl.BlockSpec(memory_space=pl.ANY)] * count
    found = pl.pallas_call(
        functools.partial(sweep, rows, cols),
        out_shape=results,
        in_specs=anywhere(1) + whole(2) + anywhere(6),
        out_specs=anywhere(3),
        scratch_shapes=[
            vmem(slab, width),
            vmem(slab, width),
            vmem(3, width, width),
            dma(5),
            vmem(cols * slab, rows * slab),
            vmem(slab, width),
            vmem(slab, width),
            square,
            square,
            square,
            vmem(2, width, width),
            dma(7),
            vmem(rows, share, packed),
        ]
        + [square] * 11
        + [
            vmem(rows, slab, 2 * width),
            vmem(cols * slab, 2 * width),
            vmem(cols, slab, 2 * width),
            vmem(slab, 2 * width),
            vmem(rows, share, 2 * slab),
            vmem(rows, share, 2 * slab),
            vmem(2 * share, rows * slab),
            vmem(share, packed),
            vmem(cols, share, packed),
            dma(4, rows),
            dma(rows),
            dma(cols),
            dma(cols),
            dma(rows),
            dma(rows),
            dma(cols),
            dma(cols),
            dma(4, rows),
            dma(rows),
        ],
        compiler_params=pltpu.CompilerParams(
            collective_id=0, has_side_effects=True, vmem_limit_bytes=56 << 20
        ),
        cost_estimate=cost,
        name="sweep",
    )(
        trail_adjoint,
        panel_one,
        panel_two,
        upstream_one,
        upstream_two,
        pivot_one,
        pivot_two,
        link_block,
        pivot_adjoint,
    )
    return pl.pallas_call(
        hand_on,
        out_shape=results,
        in_specs=anywhere(3),
        out_specs=anywhere(3),
        scratch_shapes=[dma(5)],
        compiler_params=pltpu.CompilerParams(vmem_limit_bytes=56 << 20),
        name="hand_on",
    )(*found)


def solution(mesh):
    return jax.shard_map(
        functools.partial(local, mesh.shape["row"], mesh.shape["col"]),
        mesh=mesh,
        in_specs=(
            P("row", None, "col", None),
            P(("row", "col"), None),
            P(("row", "col"), None),
            P(("row", "col"), None),
            P(("row", "col"), None),
            P(),
            P(),
            P(),
            P(),
        ),
        out_specs=(P(("row", "col"), None), P(("row", "col"), None), P()),
        check_vma=False,
    )
```
